32 devices in a mesh: req: 16 (over z, y, core), tp: 2 (over x).
Axes of the slice: x: 2, y: 2, z: 4, core: 2. Of those that a mesh axis runs over, the one named last changes fastest.
Arguments:
- hidden_in: bfloat16 [32768, 1536], P(('req', 'tp')), may hold values from -30 to 30
- segment_ids: int32 [32768], P('req'), may hold values from 0 to 9, as said below
- page_owner: int32 [512], P('req'), may hold values from 0 to 15, as said below
- norm_gain: bfloat16 [1536], replicated, may hold values from 0.099609375 to 1.8984375
- w_qkv: bfloat16 [1536, 1536], P(None, 'tp'), may hold values from -16 to 16
- w_out: bfloat16 [768, 1536], P('tp'), may hold values from -0.625 to 0.625
Outputs:
- hidden_out: bfloat16 [32768, 1536], P(('req', 'tp'))
- kv_cache: bfloat16 [512, 4, 2, 6144], P('req', 'tp')
The draws below stay inside these ranges and needn't reach their ends.
Inputs may be any that keep to these rules, and one draw needn't show every extreme that they name: `segment_ids`: within a group the numbers never fall. 0 marks the shared prefix, which comes first with 128 to 512 tokens; 1 to 8 mark the requests (a request may be empty); 9 marks padding at the end. At least three quarters of each group's tokens are not padding, and some group has none. `page_owner`: for each page number p, the 16 groups name 16 different owners for their page p. A group names one owner for at most 2 of its pages.
All inputs are finite; a program needn't handle non-finite values.
Results may differ from the reference program's by a relative error of at most 0.0095.
Values may be sent and summed in bfloat16 or wider, within the bound.
A program may use at most 128 MiB of HBM per device.

```python
import math
import jax
import jax.numpy as jnp
from jax import lax

D = 1536
HEAD = 96
HEADS_Q = 8
HEADS_KV = 4
PAGE = 64
REQS = 8
TOK_DEV = 2048
TOKENS = 32768
PAGES_DEV = 32
QKV_COLS = 1536
CACHE_PAGES = 512
N_REQ = 16
N_TP = 2


def draw_hidden_in(key, part):
    key_main, key_rows, key_cols = jax.random.split(key, 3)
    base_values = jnp.clip(jax.random.normal(key_main, (TOKENS, D), jnp.float32), -5.0, 5.0)
    row_scale = jnp.exp(jax.random.uniform(key_rows, (TOKENS, 1), jnp.float32, math.log(0.3), math.log(3.0)))
    col_scale = jnp.exp(jax.random.uniform(key_cols, (1, D), jnp.float32, math.log(0.5), math.log(2.0)))
    return (base_values * row_scale * col_scale).astype(jnp.bfloat16)


def draw_w_qkv(key, part):
    key_query, key_key, key_value = jax.random.split(key, 3)
    spread = D ** (-0.5)
    query_cols = jnp.clip(jax.random.normal(key_query, (D, HEADS_Q, HEAD), jnp.float32), -5.0, 5.0) * spread
    key_cols = jnp.clip(jax.random.normal(key_key, (D, HEADS_KV, HEAD), jnp.float32), -5.0, 5.0) * spread
    value_cols = jnp.clip(jax.random.normal(key_value, (D, HEADS_KV, HEAD), jnp.float32), -5.0, 5.0) * spread
    query_block = query_cols.reshape(D, N_TP, HEADS_Q // N_TP * HEAD)
    key_block = key_cols.reshape(D, N_TP, HEADS_KV // N_TP * HEAD)
    value_block = value_cols.reshape(D, N_TP, HEADS_KV // N_TP * HEAD)
    joined = jnp.concatenate([query_block, key_block, value_block], axis=2)
    return joined.reshape(D, QKV_COLS).astype(jnp.bfloat16)


def draw_segment_ids(key, part):
    key_full, key_live, key_prefix, key_cuts = jax.random.split(key, 4)
    full_group = jax.random.randint(key_full, (), 0, N_REQ)
    groups = jnp.arange(N_REQ, dtype=jnp.int32)
    live_len = jax.random.randint(key_live, (N_REQ,), 3 * TOK_DEV // 4, TOK_DEV + 1)
    live_len = jnp.where(groups == full_group, TOK_DEV, live_len)
    prefix_len = jax.random.randint(key_prefix, (N_REQ,), TOK_DEV // 16, TOK_DEV // 4 + 1)
    suffix_len = live_len - prefix_len
    cut_points = jax.random.randint(key_cuts, (N_REQ, REQS - 1), 0, 1 << 30)
    cut_points = prefix_len[:, None] + cut_points % suffix_len[:, None]
    token_index = jnp.arange(TOK_DEV, dtype=jnp.int32)
    counted = jnp.sum((cut_points[:, None, :] <= token_index[None, :, None]).astype(jnp.int32), axis=2)
    segments = 1 + counted
    segments = jnp.where(token_index[None, :] < prefix_len[:, None], 0, segments)
    segments = jnp.where(token_index[None, :] >= live_len[:, None], REQS + 1, segments)
    return segments.reshape(TOKENS).astype(jnp.int32)


def draw_page_owner(key, part):
    key_offset, key_owner = jax.random.split(key)
    offsets = jax.random.permutation(key_offset, N_REQ).astype(jnp.int32)
    relabel = jax.random.permutation(key_owner, N_REQ).astype(jnp.int32)
    group_index = jnp.arange(N_REQ, dtype=jnp.int32)[:, None]
    page_index = jnp.arange(PAGES_DEV, dtype=jnp.int32)[None, :]
    shifted = (group_index + offsets[page_index % N_REQ]) % N_REQ
    return relabel[shifted].reshape(CACHE_PAGES).astype(jnp.int32)


def level_of(rng, dims, pieces, least, largest):
    level, own = 1.0, jax.random.fold_in(rng, 6)
    for dim, parts in pieces:
        draws = jnp.exp(jax.random.uniform(jax.random.fold_in(own, dim), (parts,), jnp.float32, least / len(pieces), largest / len(pieces)))
        level = level * jnp.repeat(draws, dims[dim] // parts).reshape([-1 if axis == dim else 1 for axis in range(len(dims))])
    return level


def noise(rng, dims, scale, reach, shards=(), kind=jnp.bfloat16):
    factor_of = level_of(rng, dims, shards, -0.22, 0.18) if shards else 1.0
    values = jax.random.normal(rng, dims, jnp.float32) * scale * factor_of
    return jnp.minimum(jnp.maximum(values, -reach), reach).astype(kind)


def setup_inputs(seed: int = 0) -> dict:
    arg_keys = jax.random.split(jax.random.key(seed), 7)
    return {
        "hidden_in": draw_hidden_in(jax.random.fold_in(arg_keys[6], 71), 0),
        "segment_ids": draw_segment_ids(jax.random.fold_in(arg_keys[6], 71), 0),
        "page_owner": draw_page_owner(jax.random.fold_in(arg_keys[6], 71), 0),
        "norm_gain": jnp.clip(1.0 + 0.18 * jax.random.normal(arg_keys[3], (D,), jnp.float32), 0.099609375, 1.8984375).astype(jnp.bfloat16),
        "w_qkv": draw_w_qkv(jax.random.fold_in(arg_keys[6], 71), 0),
        "w_out": noise(arg_keys[5], (HEADS_Q * HEAD, D), HEAD ** -0.5, 0.625, ((0, 2),)),
    }


rotary_base = 100000.0
norm_eps = 1e-05
masked_score = -1e+30

def positions_of(segments):
    length = segments.shape[0]
    counter = jnp.arange(length, dtype=jnp.int32)
    previous = jnp.concatenate([segments[:1] - 1, segments[:-1]])
    starts = lax.cummax(jnp.where(segments != previous, counter, 0), axis=0)
    prefix_len = jnp.sum((segments == 0).astype(jnp.int32))
    return counter - starts + jnp.where(segments > 0, prefix_len, 0)

def rotary_tables(positions, width):
    half_width = width // 2
    exponent = jnp.arange(half_width, dtype=jnp.float32) * (2.0 / width)
    inverse = jnp.power(jnp.float32(rotary_base), -exponent)
    angles = positions.astype(jnp.float32)[:, None] * inverse[None, :]
    return (jnp.cos(angles), jnp.sin(angles))

def rotate(vectors, cosine, sine_table):
    half_width = vectors.shape[-1] // 2
    front_half = vectors[..., :half_width]
    second = vectors[..., half_width:]
    cosine = cosine[:, None, :]
    sine_table = sine_table[:, None, :]
    return jnp.concatenate([front_half * cosine - second * sine_table, second * cosine + front_half * sine_table], axis=-1)

def normalize(token_rows, gain_vector):
    values = token_rows.astype(jnp.float32)
    inverse_root = lax.rsqrt(lax.optimization_barrier(jnp.mean(values * values, axis=-1, keepdims=True)) + norm_eps)
    return (values * inverse_root * gain_vector.astype(jnp.float32)).astype(jnp.bfloat16)

def dense_attention(queries, key_vectors, value_vectors, segments):
    row_count = queries.shape[0]
    group_ratio = HEADS_Q // HEADS_KV
    places = jnp.arange(row_count, dtype=jnp.int32)
    allowed = (places[None, :] <= places[:, None]) & ((segments[None, :] == segments[:, None]) | (segments[None, :] == 0))
    wide_keys = jnp.repeat(key_vectors.astype(jnp.float32), group_ratio, axis=1)
    wide_values = jnp.repeat(value_vectors.astype(jnp.float32), group_ratio, axis=1)
    raw_scores = jnp.einsum('qhd,khd->hqk', queries.astype(jnp.float32), wide_keys) * HEAD ** (-0.5)
    row_max = lax.optimization_barrier(jnp.max(jnp.where(allowed, raw_scores, masked_score), axis=-1, keepdims=True))
    weights = jnp.where(allowed, jnp.exp(raw_scores - row_max), 0.0)
    totals = lax.optimization_barrier(jnp.sum(weights, axis=-1))
    rounded = weights.astype(jnp.bfloat16)
    rounded = lax.optimization_barrier(rounded)
    mixed_sum = jnp.einsum('hqk,khd->qhd', rounded.astype(jnp.float32), wide_values)
    result = mixed_sum / jnp.transpose(totals)[:, :, None]
    return result.astype(jnp.bfloat16).reshape(row_count, HEADS_Q * HEAD)

def reference(hidden_in, segment_ids, page_owner, norm_gain, w_qkv, w_out):
    query_width = HEADS_Q // N_TP * HEAD
    kv_width = HEADS_KV // N_TP * HEAD
    per_block = query_width + 2 * kv_width
    blocked = w_qkv.reshape(D, N_TP, per_block)
    w_query = blocked[:, :, :query_width].reshape(D, HEADS_Q * HEAD)
    w_key = blocked[:, :, query_width:query_width + kv_width].reshape(D, HEADS_KV * HEAD)
    w_value = blocked[:, :, query_width + kv_width:].reshape(D, HEADS_KV * HEAD)

    def group_layer(inputs):
        token_rows, segments = inputs
        normed = normalize(token_rows, norm_gain)
        positions = positions_of(segments)
        cosine, sine_table = rotary_tables(positions, HEAD)
        queries = jnp.dot(normed, w_query, preferred_element_type=jnp.float32).reshape(TOK_DEV, HEADS_Q, HEAD)
        queries = rotate(queries, cosine, sine_table).astype(jnp.bfloat16)
        key_vectors = jnp.dot(normed, w_key, preferred_element_type=jnp.float32).reshape(TOK_DEV, HEADS_KV, HEAD)
        key_vectors = rotate(key_vectors, cosine, sine_table).astype(jnp.bfloat16)
        value_vectors = jnp.dot(normed, w_value, preferred_element_type=jnp.float32).astype(jnp.bfloat16).reshape(TOK_DEV, HEADS_KV, HEAD)
        queries, key_vectors, value_vectors = lax.optimization_barrier((queries, key_vectors, value_vectors))
        attended = dense_attention(queries, key_vectors, value_vectors, segments)
        projected = jnp.dot(attended, w_out, preferred_element_type=jnp.float32)
        result = (token_rows.astype(jnp.float32) + projected).astype(jnp.bfloat16)
        key_pages = key_vectors.reshape(PAGES_DEV, PAGE, HEADS_KV, HEAD).transpose(0, 2, 1, 3).reshape(PAGES_DEV, HEADS_KV, PAGE * HEAD)
        value_pages = value_vectors.reshape(PAGES_DEV, PAGE, HEADS_KV, HEAD).transpose(0, 2, 1, 3).reshape(PAGES_DEV, HEADS_KV, PAGE * HEAD)
        return (result, jnp.stack([key_pages, value_pages], axis=2))
    rows_all = hidden_in.reshape(N_REQ, TOK_DEV, D)
    segments_all = segment_ids.reshape(N_REQ, TOK_DEV)
    results, page_blocks = lax.map(group_layer, (rows_all, segments_all))
    live_pages = segments_all[:, ::PAGE] != REQS + 1
    owners = page_owner.reshape(N_REQ, PAGES_DEV)
    page_numbers = jnp.arange(PAGES_DEV, dtype=jnp.int32)[None, :]
    targets = jnp.where(live_pages, owners * PAGES_DEV + page_numbers, CACHE_PAGES).astype(jnp.int32)
    cache_rows = jnp.zeros((CACHE_PAGES, HEADS_KV, 2, PAGE * HEAD), jnp.bfloat16)
    cache_rows = cache_rows.at[targets.reshape(CACHE_PAGES)].set(page_blocks.reshape(CACHE_PAGES, HEADS_KV, 2, PAGE * HEAD), mode='drop')
    return (results.reshape(TOKENS, D), cache_rows)
```

```python
import jax
import jax.numpy as jnp
from jax import lax
from jax.experimental import pallas as pl
from jax.experimental.pallas import tpu as pltpu
from jax.sharding import PartitionSpec as P

HEAD = 96
HEADS_Q = 8
HEADS_KV = 4
PAGE = 64
REQS = 8


rotary_base = 100000.0
norm_eps = 1e-05
masked_score = -1e30


def rotary_tables(positions, width):
    half_width = width // 2
    exponent = jnp.arange(half_width, dtype=jnp.float32) * (2.0 / width)
    inverse = jnp.power(jnp.float32(rotary_base), -exponent)
    angles = positions.astype(jnp.float32)[:, None] * inverse[None, :]
    return (jnp.cos(angles), jnp.sin(angles))


def rotate(vectors, cosine, sine_table):
    half_width = vectors.shape[-1] // 2
    front_half = vectors[..., :half_width]
    second = vectors[..., half_width:]
    cosine = cosine[:, None, :]
    sine_table = sine_table[:, None, :]
    return jnp.concatenate(
        [front_half * cosine - second * sine_table, second * cosine + front_half * sine_table],
        axis=-1,
    )


def normalize(token_rows, gain_vector):
    values = token_rows.astype(jnp.float32)
    inverse_root = lax.rsqrt(jnp.mean(values * values, axis=-1, keepdims=True) + norm_eps)
    return (values * inverse_root * gain_vector.astype(jnp.float32)).astype(jnp.bfloat16)


Q_BLOCK = 256
K_BLOCK = 256
PIECES = 3


def weights_kernel(wq_ref, wo_ref, oq_ref, oo_ref, send_sem, recv_sem):
    req = lax.axis_index("req")
    tp = lax.axis_index("tp")
    member = lax.rem(req, 4)
    base = req - member
    core_member = member + 1 - 2 * lax.rem(member, 2)
    row_member = member + 2 - 4 * (member // 2)
    across = {"tp": 1 - tp}
    core_peer = {"req": base + core_member}
    row_peer = {"req": base + row_member}
    barrier = pltpu.get_barrier_semaphore()
    for peer in (across, core_peer, row_peer):
        pl.semaphore_signal(barrier, inc=1, device_id=peer, device_id_type=pl.DeviceIdType.MESH)
    pl.semaphore_wait(barrier, 3)

    q_rows = wq_ref.shape[0] // 4 // PIECES
    o_rows = wo_ref.shape[0] // 4

    def views(ref_q, ref_o, owner, piece):
        if piece < PIECES:
            return ref_q.at[pl.ds((owner * PIECES + piece) * q_rows, q_rows)]
        return ref_o.at[pl.ds(owner * o_rows, o_rows)]

    def copy(source, owner, piece, channel, peer):
        src = views(*source, owner, piece)
        dst = views(oq_ref, oo_ref, owner, piece)
        return pltpu.make_async_remote_copy(
            src_ref=src,
            dst_ref=dst,
            send_sem=send_sem.at[piece, channel],
            recv_sem=recv_sem.at[piece, channel],
            device_id=peer,
            device_id_type=pl.DeviceIdType.MESH,
        )

    here = (oq_ref, oo_ref)
    pieces = range(PIECES + 1)
    first = [copy((wq_ref, wo_ref), member, p, 0, across) for p in pieces]
    core_first = [copy(here, member, p, 1, core_peer) for p in pieces]
    row_first = [copy(here, member, p, 2, row_peer) for p in pieces]
    core_second = [copy(here, row_member, p, 3, core_peer) for p in pieces]
    for c in first:
        c.start()
    for p in pieces:
        first[p].wait_recv()
        row_first[p].start()
        core_first[p].start()
        if p >= 1:
            row_first[p - 1].wait_recv()
            core_second[p - 1].start()
    row_first[PIECES].wait_recv()
    core_second[PIECES].start()
    for p in pieces:
        first[p].wait_send()
        row_first[p].wait_send()
        core_first[p].wait()
        core_second[p].wait()


def other_weights(w_qkv, w_out):
    return pl.pallas_call(
        weights_kernel,
        out_shape=(
            jax.ShapeDtypeStruct(w_qkv.shape, w_qkv.dtype),
            jax.ShapeDtypeStruct(w_out.shape, w_out.dtype),
        ),
        in_specs=[pl.BlockSpec(memory_space=pl.ANY)] * 2,
        out_specs=[pl.BlockSpec(memory_space=pl.ANY)] * 2,
        scratch_shapes=[
            pltpu.SemaphoreType.DMA((PIECES + 1, 4)),
            pltpu.SemaphoreType.DMA((PIECES + 1, 4)),
        ],
        compiler_params=pltpu.CompilerParams(collective_id=0, has_side_effects=True),
        name="weights",
    )(w_qkv, w_out)


def attention_kernel(
    info_ref, blocks_ref, q_ref, kv_ref, starts_ref, wo_own_ref, wo_other_ref, hidden_ref, out_ref, mixed_ref
):
    block = pl.program_id(0)
    row_offset = info_ref[0]
    prefix = info_ref[1]
    key_offset = info_ref[2]
    prefix_end = blocks_ref[0, block]
    low = blocks_ref[1, block]
    high = blocks_ref[2, block]
    factor = HEAD ** (-0.5) * 1.4426950408889634
    local = lax.broadcasted_iota(jnp.int32, (Q_BLOCK, 1), 0) + row_offset + block * Q_BLOCK
    places = jnp.concatenate([local, local], axis=0)
    starts = starts_ref[...]
    starts = jnp.concatenate([starts, starts], axis=0)
    for head in range(HEADS_KV):
        key_row = (head // 2) * 4 + head % 2
        queries = q_ref[2 * head : 2 * head + 2].reshape(2 * Q_BLOCK, HEAD)

        def step(number, carry):
            row_max, totals, mixed = carry
            begin = pl.multiple_of(number * K_BLOCK + key_offset, K_BLOCK)
            keys = kv_ref[key_row, pl.ds(begin, K_BLOCK), :]
            values = kv_ref[key_row + 2, pl.ds(begin, K_BLOCK), :]
            scores = lax.dot_general(
                queries, keys, (((1,), (1,)), ((), ())), preferred_element_type=jnp.float32
            ) * factor
            key_places = lax.broadcasted_iota(jnp.int32, (1, K_BLOCK), 1) + number * K_BLOCK
            allowed = (key_places <= places) & ((key_places >= starts) | (key_places < prefix))
            scores = jnp.where(allowed, scores, masked_score)
            new_max = jnp.maximum(row_max, jnp.max(scores, axis=1, keepdims=True))
            weights = jnp.exp2(scores - new_max)
            scale = jnp.exp2(row_max - new_max)
            totals = totals * scale + jnp.sum(weights, axis=1, keepdims=True)
            mixed = mixed * scale + jnp.dot(
                weights.astype(jnp.bfloat16), values, preferred_element_type=jnp.float32
            )
            return new_max, totals, mixed

        carry = (
            jnp.full((2 * Q_BLOCK, 1), -1e20, jnp.float32),
            jnp.zeros((2 * Q_BLOCK, 1), jnp.float32),
            jnp.zeros((2 * Q_BLOCK, HEAD), jnp.float32),
        )
        carry = lax.fori_loop(0, prefix_end, step, carry)
        _, totals, mixed = lax.fori_loop(low, high, step, carry)
        result = (mixed / totals).astype(jnp.bfloat16)
        mixed_ref[:, 2 * head * HEAD : (2 * head + 1) * HEAD] = result[:Q_BLOCK]
        mixed_ref[:, (2 * head + 1) * HEAD : (2 * head + 2) * HEAD] = result[Q_BLOCK:]
    half = HEADS_Q * HEAD // 2
    product = jnp.dot(mixed_ref[:, :half], wo_own_ref[...], preferred_element_type=jnp.float32)
    product += jnp.dot(mixed_ref[:, half:], wo_other_ref[...], preferred_element_type=jnp.float32)
    out_ref[...] = (hidden_ref[...].astype(jnp.float32) + product).astype(jnp.bfloat16)


def attention(info, blocks, queries, keys_values, starts, wo_own, wo_other, hidden):
    tokens, width = hidden.shape
    whole = lambda shape: pl.BlockSpec(shape, lambda i, *_: (0,) * len(shape))
    return pl.pallas_call(
        attention_kernel,
        grid_spec=pltpu.PrefetchScalarGridSpec(
            num_scalar_prefetch=2,
            grid=(tokens // Q_BLOCK,),
            in_specs=[
                pl.BlockSpec((HEADS_Q, Q_BLOCK, HEAD), lambda i, *_: (0, i, 0)),
                whole(keys_values.shape),
                pl.BlockSpec((Q_BLOCK, 1), lambda i, *_: (i, 0)),
                whole(wo_own.shape),
                whole(wo_other.shape),
                pl.BlockSpec((Q_BLOCK, width), lambda i, *_: (i, 0)),
            ],
            out_specs=pl.BlockSpec((Q_BLOCK, width), lambda i, *_: (i, 0)),
            scratch_shapes=[pltpu.VMEM((Q_BLOCK, HEADS_Q * HEAD), jnp.bfloat16)],
        ),
        out_shape=jax.ShapeDtypeStruct(hidden.shape, hidden.dtype),
        compiler_params=pltpu.CompilerParams(vmem_limit_bytes=48 * 1024 * 1024),
        cost_estimate=pl.CostEstimate(
            flops=20_000_000_000, bytes_accessed=16_000_000, transcendentals=8_000_000
        ),
        name="attention",
    )(info, blocks, queries, keys_values, starts, wo_own, wo_other, hidden)


def heads_of(projected, cosine, sine_table):
    tokens = projected.shape[0]
    local_query, local_kv = HEADS_Q // 2, HEADS_KV // 2
    turned = rotate(
        projected[:, : (local_query + local_kv) * HEAD].reshape(tokens, -1, HEAD), cosine, sine_table
    ).astype(jnp.bfloat16)
    values = projected[:, (local_query + local_kv) * HEAD :].reshape(tokens, local_kv, HEAD)
    return (
        turned[:, :local_query],
        jnp.concatenate([turned[:, local_query:], values.astype(jnp.bfloat16)], axis=1).reshape(tokens, -1),
    )


def shards(hidden_in, segment_ids, page_owner, norm_gain, w_qkv, w_out):
    req_count = lax.axis_size("req")
    tp = lax.axis_index("tp")
    group_len = segment_ids.shape[0]
    tokens = hidden_in.shape[0]
    local_kv = HEADS_KV // 2
    row_offset = tp * tokens
    numbers = jnp.arange(REQS + 2, dtype=jnp.int32)
    firsts = jnp.sum((segment_ids[None, :] < numbers[:, None]).astype(jnp.int32), axis=1)
    prefix = firsts[1]
    own_segments = lax.dynamic_slice(segment_ids, (row_offset,), (tokens,))
    starts = jnp.sum(
        jnp.where(own_segments[:, None] == numbers[None, :], firsts[None, :], 0), axis=1
    )
    places = row_offset + jnp.arange(tokens, dtype=jnp.int32)
    positions = places - starts + jnp.where(own_segments > 0, prefix, 0)
    cosine, sine_table = rotary_tables(positions, HEAD)
    wq_other, wo_other = other_weights(w_qkv, w_out)
    normed = normalize(hidden_in, norm_gain)
    queries_own, kv_own = heads_of(
        jnp.dot(normed, w_qkv, preferred_element_type=jnp.float32), cosine, sine_table
    )
    queries_other, kv_other = heads_of(
        jnp.dot(normed, wq_other, preferred_element_type=jnp.float32), cosine, sine_table
    )
    peer_own = lax.ppermute(kv_other, "tp", [(0, 1), (1, 0)])
    peer_other = lax.ppermute(kv_own, "tp", [(0, 1)])
    cached = jnp.concatenate([peer_own, kv_own], axis=0)
    keys_values = jnp.concatenate(
        [cached, jnp.concatenate([peer_other, kv_other], axis=0)], axis=1
    )
    keys_values = keys_values.reshape(group_len, 2 * HEADS_KV, HEAD).transpose(1, 0, 2)
    queries = jnp.concatenate([queries_own, queries_other], axis=1).transpose(1, 0, 2)

    block_count = tokens // Q_BLOCK
    block_numbers = jnp.arange(block_count, dtype=jnp.int32)
    high = (row_offset + (block_numbers + 1) * Q_BLOCK) // K_BLOCK
    prefix_end = jnp.minimum((prefix + K_BLOCK - 1) // K_BLOCK, high)
    low = jnp.maximum(starts[::Q_BLOCK] // K_BLOCK, prefix_end)
    blocks = jnp.stack([prefix_end, low, high])
    info = jnp.stack([row_offset, prefix, (1 - tp) * tokens])

    page_count = group_len // PAGE
    lane_count = -(-page_count // req_count)
    page_numbers = jnp.arange(page_count, dtype=jnp.int32)
    live_pages = segment_ids[::PAGE] != REQS + 1
    half_pages = page_count // 2
    swap = lambda x: jnp.where(tp == 0, jnp.roll(x, half_pages), x)
    local_numbers, local_owner, local_live = swap(page_numbers), swap(page_owner), swap(live_pages)
    page_data = (
        cached.reshape(page_count, PAGE, 2, local_kv, HEAD)
        .transpose(0, 3, 2, 1, 4)
        .reshape(page_count, local_kv * 2 * PAGE * HEAD)
    )
    same_owner = (
        (local_owner[:, None] == local_owner[None, :])
        & local_live[None, :]
        & (local_numbers[None, :] < local_numbers[:, None])
    )
    page_rank = jnp.sum(same_owner.astype(jnp.int32), axis=1)
    owner_ids = jnp.arange(req_count, dtype=jnp.int32)
    lane_ids = jnp.arange(lane_count, dtype=jnp.int32)
    selection = (
        (local_owner[None, None, :] == owner_ids[:, None, None])
        & (page_rank[None, None, :] == lane_ids[None, :, None])
        & local_live[None, None, :]
    )
    send_pages = jnp.einsum(
        "olp,pc->olc", selection.astype(jnp.bfloat16), page_data, preferred_element_type=jnp.float32
    ).astype(jnp.bfloat16)
    send_ids = jnp.sum(jnp.where(selection, local_numbers[None, None, :] + 1, 0), axis=2) - 1
    received_ids = lax.all_to_all(send_ids, "req", split_axis=0, concat_axis=0, tiled=True)
    received = lax.all_to_all(send_pages, "req", split_axis=0, concat_axis=0, tiled=True)
    hidden_out = attention(info, blocks, queries, keys_values, starts[:, None], w_out, wo_other, hidden_in)
    placing = (
        received_ids.reshape(req_count * lane_count)[None, :] == page_numbers[:, None]
    ).astype(jnp.bfloat16)
    cache_rows = jnp.dot(
        placing,
        received.reshape(req_count * lane_count, local_kv * 2 * PAGE * HEAD),
        preferred_element_type=jnp.float32,
    ).astype(jnp.bfloat16)
    return (hidden_out, cache_rows.reshape(page_count, local_kv, 2, PAGE * HEAD))


def solution(mesh):
    placed = (P(("req", "tp"), None), P("req"), P("req"), P(), P(None, "tp"), P("tp", None))
    return jax.shard_map(
        shards,
        mesh=mesh,
        in_specs=placed,
        out_specs=(P(("req", "tp"), None), P("req", "tp", None, None)),
        check_vma=False,
    )
```

```python
import jax
import jax.numpy as jnp
from jax import lax
from jax.experimental import pallas as pl
from jax.experimental.pallas import tpu as pltpu
from jax.sharding import PartitionSpec as P

HEAD = 96
HEADS_Q = 8
HEADS_KV = 4
PAGE = 64
REQS = 8


rotary_base = 100000.0
norm_eps = 1e-05
masked_score = -1e30


def rotary_tables(positions, width):
    half_width = width // 2
    exponent = jnp.arange(half_width, dtype=jnp.float32) * (2.0 / width)
    inverse = jnp.power(jnp.float32(rotary_base), -exponent)
    angles = positions.astype(jnp.float32)[:, None] * inverse[None, :]
    return (jnp.cos(angles), jnp.sin(angles))


def normalize(token_rows, gain_vector):
    values = token_rows.astype(jnp.float32)
    inverse_root = lax.rsqrt(jnp.mean(values * values, axis=-1, keepdims=True) + norm_eps)
    return (values * inverse_root * gain_vector.astype(jnp.float32)).astype(jnp.bfloat16)


Q_BLOCK = 256
K_BLOCK = 256
PIECES = 3


def project_kernel(
    hidden_ref, gain_ref, cosine_ref, sine_ref, wq_ref, wo_ref,
    q_own_ref, kv_own_ref, q_other_ref, kv_other_ref, wo_other_ref, peer_own_ref, peer_other_ref,
    wq_other_ref, normed_ref, cos_ref, left_ref, right_ref, send_sem, recv_sem, kv_send, kv_recv,
):
    req = lax.axis_index("req")
    tp = lax.axis_index("tp")
    member = lax.rem(req, 4)
    base = req - member
    core_member = member + 1 - 2 * lax.rem(member, 2)
    row_member = member + 2 - 4 * (member // 2)
    across = {"tp": 1 - tp}
    core_peer = {"req": base + core_member}
    row_peer = {"req": base + row_member}
    barrier = pltpu.get_barrier_semaphore()
    for peer in (across, core_peer, row_peer):
        pl.semaphore_signal(barrier, inc=1, device_id=peer, device_id_type=pl.DeviceIdType.MESH)
    pl.semaphore_wait(barrier, 3)

    q_rows = wq_ref.shape[0] // 4 // PIECES
    o_rows = wo_ref.shape[0] // 4

    def remote(src, dst, sends, receives, peer):
        return pltpu.make_async_remote_copy(
            src_ref=src, dst_ref=dst, send_sem=sends, recv_sem=receives,
            device_id=peer, device_id_type=pl.DeviceIdType.MESH,
        )

    def views(ref_q, ref_o, owner, piece):
        if piece < PIECES:
            return ref_q.at[pl.ds((owner * PIECES + piece) * q_rows, q_rows)]
        return ref_o.at[pl.ds(owner * o_rows, o_rows)]

    def copy(source, owner, piece, channel, peer):
        return remote(
            views(*source, owner, piece), views(wq_other_ref, wo_other_ref, owner, piece),
            send_sem.at[piece, channel], recv_sem.at[piece, channel], peer,
        )

    here = (wq_other_ref, wo_other_ref)
    pieces = range(PIECES + 1)
    first = [copy((wq_ref, wo_ref), member, p, 0, across) for p in pieces]
    core_first = [copy(here, member, p, 1, core_peer) for p in pieces]
    row_first = [copy(here, member, p, 2, row_peer) for p in pieces]
    core_second = [copy(here, row_member, p, 3, core_peer) for p in pieces]
    tokens = hidden_ref.shape[0]
    blocks = tokens // Q_BLOCK
    width = cos_ref.shape[1]
    half = HEAD // 2

    def kv_copy(source, target, which, block):
        rows = pl.ds(block * Q_BLOCK, Q_BLOCK)
        return remote(
            source.at[rows], target.at[rows], kv_send.at[which, block], kv_recv.at[which, block], across
        )

    own_copies = [kv_copy(kv_own_ref, peer_other_ref, 0, b) for b in range(blocks)]
    other_copies = [kv_copy(kv_other_ref, peer_own_ref, 1, b) for b in range(blocks)]

    for p in range(PIECES):
        first[p].start()

    def project(rows, weight_ref, q_ref, kv_ref):
        normed = normed_ref[rows, :]
        cosine, left, right = cos_ref[rows, :], left_ref[rows, :], right_ref[rows, :]

        def turn(x):
            return (
                x * cosine
                + pltpu.roll(x, width - half, 1) * left
                + pltpu.roll(x, half, 1) * right
            )

        q = jnp.dot(normed, weight_ref[:, :width], preferred_element_type=jnp.float32)
        q_ref[rows, :] = turn(q).astype(jnp.bfloat16)
        kv = jnp.dot(normed, weight_ref[:, width:], preferred_element_type=jnp.float32)
        lanes = lax.broadcasted_iota(jnp.int32, kv.shape, 1)
        kv_ref[rows, :] = jnp.where(lanes < width // 2, turn(kv), kv).astype(jnp.bfloat16)

    def own(block):
        rows = pl.ds(block * Q_BLOCK, Q_BLOCK)
        normed_ref[rows, :] = normalize(hidden_ref[rows, :], gain_ref[...])
        cosine, sine = cosine_ref[rows, :], sine_ref[rows, :]
        nothing = jnp.zeros_like(sine)
        for piece in range(width // half):
            lanes = slice(piece * half, (piece + 1) * half)
            cos_ref[rows, lanes] = cosine
            left_ref[rows, lanes] = nothing if piece % 2 else -sine
            right_ref[rows, lanes] = sine if piece % 2 else nothing
        project(rows, wq_ref, q_own_ref, kv_own_ref)

    def forward(p):
        first[p].wait_recv()
        row_first[p].start()
        core_first[p].start()

    for block in range(blocks):
        own(block)
        if block >= 1:
            forward(block - 1)
        own_copies[block].start()
    first[PIECES].start()
    for p in range(PIECES):
        row_first[p].wait_recv()
        core_second[p].start()
    for p in range(PIECES):
        core_first[p].wait_recv()
        core_second[p].wait_recv()
    for block in range(blocks):
        project(pl.ds(block * Q_BLOCK, Q_BLOCK), wq_other_ref, q_other_ref, kv_other_ref)
        other_copies[block].start()
        if block == 1:
            forward(PIECES)
    row_first[PIECES].wait_recv()
    core_second[PIECES].start()
    core_first[PIECES].wait_recv()
    core_second[PIECES].wait_recv()
    for p in pieces:
        for c in (first[p], row_first[p], core_first[p], core_second[p]):
            c.wait_send()
    for c in own_copies + other_copies:
        c.wait()


def project(hidden, gain, cosine, sine, w_qkv, w_out):
    tokens, width = hidden.shape
    part = w_qkv.shape[1] // 2
    blocks = tokens // Q_BLOCK
    vmem = pl.BlockSpec(memory_space=pltpu.VMEM)
    anywhere = pl.BlockSpec(memory_space=pl.ANY)
    share = jax.ShapeDtypeStruct((tokens, part), jnp.bfloat16)
    return pl.pallas_call(
        project_kernel,
        out_shape=(share,) * 4 + (jax.ShapeDtypeStruct(w_out.shape, w_out.dtype),) + (share,) * 2,
        in_specs=[vmem] * 5 + [anywhere],
        out_specs=[vmem] * 4 + [anywhere] * 3,
        scratch_shapes=[
            pltpu.VMEM(w_qkv.shape, w_qkv.dtype),
            pltpu.VMEM((tokens, width), jnp.bfloat16),
            pltpu.VMEM((tokens, part), jnp.float32),
            pltpu.VMEM((tokens, part), jnp.float32),
            pltpu.VMEM((tokens, part), jnp.float32),
            pltpu.SemaphoreType.DMA((PIECES + 1, 4)),
            pltpu.SemaphoreType.DMA((PIECES + 1, 4)),
            pltpu.SemaphoreType.DMA((2, blocks)),
            pltpu.SemaphoreType.DMA((2, blocks)),
        ],
        compiler_params=pltpu.CompilerParams(
            collective_id=0, has_side_effects=True, vmem_limit_bytes=48 * 1024 * 1024
        ),
        cost_estimate=pl.CostEstimate(
            flops=5_000_000_000, bytes_accessed=16_000_000, transcendentals=1024
        ),
        name="project",
    )(hidden, gain, cosine, sine, w_qkv, w_out)


def attention_kernel(
    info_ref, blocks_ref, q_own_ref, q_other_ref, peer_own_ref, kv_own_ref, peer_other_ref, kv_other_ref,
    starts_ref, wo_own_ref, wo_other_ref, hidden_ref, out_ref, mixed_ref, kv_ref
):
    block = pl.program_id(0)

    @pl.when(block == 0)
    def _():
        tokens = kv_own_ref.shape[0]
        sources = ((peer_own_ref, kv_own_ref), (peer_other_ref, kv_other_ref))
        for group in range(2):
            for part in range(2):
                for head in range(4):
                    kv_ref[group * 4 + head, part * tokens : (part + 1) * tokens, :] = sources[group][
                        part
                    ][:, head * HEAD : (head + 1) * HEAD]

    row_offset = info_ref[0]
    prefix = info_ref[1]
    key_offset = info_ref[2]
    prefix_end = blocks_ref[0, block]
    low = blocks_ref[1, block]
    high = blocks_ref[2, block]
    factor = HEAD ** (-0.5) * 1.4426950408889634
    local = lax.broadcasted_iota(jnp.int32, (Q_BLOCK, 1), 0) + row_offset + block * Q_BLOCK
    places = jnp.concatenate([local, local], axis=0)
    starts = starts_ref[...]
    starts = jnp.concatenate([starts, starts], axis=0)
    for head in range(HEADS_KV):
        key_row = (head // 2) * 4 + head % 2
        q_ref = q_own_ref if head < 2 else q_other_ref
        lane = (head % 2) * 2 * HEAD
        queries = jnp.concatenate(
            [q_ref[:, lane : lane + HEAD], q_ref[:, lane + HEAD : lane + 2 * HEAD]], axis=0
        )

        def step(number, carry):
            row_max, totals, mixed = carry
            begin = pl.multiple_of(number * K_BLOCK + key_offset, K_BLOCK)
            keys = kv_ref[key_row, pl.ds(begin, K_BLOCK), :]
            values = kv_ref[key_row + 2, pl.ds(begin, K_BLOCK), :]
            scores = lax.dot_general(
                queries, keys, (((1,), (1,)), ((), ())), preferred_element_type=jnp.float32
            ) * factor
            key_places = lax.broadcasted_iota(jnp.int32, (1, K_BLOCK), 1) + number * K_BLOCK
            allowed = (key_places <= places) & ((key_places >= starts) | (key_places < prefix))
            scores = jnp.where(allowed, scores, masked_score)
            new_max = jnp.maximum(row_max, jnp.max(scores, axis=1, keepdims=True))
            weights = jnp.exp2(scores - new_max)
            scale = jnp.exp2(row_max - new_max)
            totals = totals * scale + jnp.sum(weights, axis=1, keepdims=True)
            mixed = mixed * scale + jnp.dot(
                weights.astype(jnp.bfloat16), values, preferred_element_type=jnp.float32
            )
            return new_max, totals, mixed

        carry = (
            jnp.full((2 * Q_BLOCK, 1), -1e20, jnp.float32),
            jnp.zeros((2 * Q_BLOCK, 1), jnp.float32),
            jnp.zeros((2 * Q_BLOCK, HEAD), jnp.float32),
        )
        carry = lax.fori_loop(0, prefix_end, step, carry)
        _, totals, mixed = lax.fori_loop(low, high, step, carry)
        result = (mixed / totals).astype(jnp.bfloat16)
        mixed_ref[:, 2 * head * HEAD : (2 * head + 1) * HEAD] = result[:Q_BLOCK]
        mixed_ref[:, (2 * head + 1) * HEAD : (2 * head + 2) * HEAD] = result[Q_BLOCK:]
    half = HEADS_Q * HEAD // 2
    product = jnp.dot(mixed_ref[:, :half], wo_own_ref[...], preferred_element_type=jnp.float32)
    product += jnp.dot(mixed_ref[:, half:], wo_other_ref[...], preferred_element_type=jnp.float32)
    out_ref[...] = (hidden_ref[...].astype(jnp.float32) + product).astype(jnp.bfloat16)


def attention(info, blocks, queries, keys_values, starts, wo_own, wo_other, hidden):
    tokens, width = hidden.shape
    half = queries[0].shape[1]
    whole = lambda shape: pl.BlockSpec(shape, lambda i, *_: (0,) * len(shape))
    return pl.pallas_call(
        attention_kernel,
        grid_spec=pltpu.PrefetchScalarGridSpec(
            num_scalar_prefetch=2,
            grid=(tokens // Q_BLOCK,),
            in_specs=[
                pl.BlockSpec((Q_BLOCK, half), lambda i, *_: (i, 0)),
                pl.BlockSpec((Q_BLOCK, half), lambda i, *_: (i, 0)),
                whole((tokens, half)),
                whole((tokens, half)),
                whole((tokens, half)),
                whole((tokens, half)),
                pl.BlockSpec((Q_BLOCK, 1), lambda i, *_: (i, 0)),
                whole(wo_own.shape),
                whole(wo_other.shape),
                pl.BlockSpec((Q_BLOCK, width), lambda i, *_: (i, 0)),
            ],
            out_specs=pl.BlockSpec((Q_BLOCK, width), lambda i, *_: (i, 0)),
            scratch_shapes=[
                pltpu.VMEM((Q_BLOCK, HEADS_Q * HEAD), jnp.bfloat16),
                pltpu.VMEM((2 * HEADS_KV, 2 * tokens, HEAD), jnp.bfloat16),
            ],
        ),
        out_shape=jax.ShapeDtypeStruct(hidden.shape, hidden.dtype),
        compiler_params=pltpu.CompilerParams(vmem_limit_bytes=48 * 1024 * 1024),
        cost_estimate=pl.CostEstimate(
            flops=20_000_000_000, bytes_accessed=16_000_000, transcendentals=8_000_000
        ),
        name="attention",
    )(info, blocks, *queries, *keys_values, starts, wo_own, wo_other, hidden)


def shards(hidden_in, segment_ids, page_owner, norm_gain, w_qkv, w_out):
    req_count = lax.axis_size("req")
    tp = lax.axis_index("tp")
    group_len = segment_ids.shape[0]
    tokens = hidden_in.shape[0]
    local_kv = HEADS_KV // 2
    row_offset = tp * tokens
    numbers = jnp.arange(REQS + 2, dtype=jnp.int32)
    firsts = jnp.sum((segment_ids[None, :] < numbers[:, None]).astype(jnp.int32), axis=1)
    prefix = firsts[1]
    own_segments = lax.dynamic_slice(segment_ids, (row_offset,), (tokens,))
    starts = jnp.sum(
        jnp.where(own_segments[:, None] == numbers[None, :], firsts[None, :], 0), axis=1
    )
    places = row_offset + jnp.arange(tokens, dtype=jnp.int32)
    positions = places - starts + jnp.where(own_segments > 0, prefix, 0)
    cosine, sine_table = rotary_tables(positions, HEAD)
    q_own, kv_own, q_other, kv_other, wo_other, peer_own, peer_other = project(
        hidden_in, norm_gain[None, :], cosine, sine_table, w_qkv, w_out
    )
    queries = (q_own, q_other)
    keys_values = (peer_own, kv_own, peer_other, kv_other)
    cached = jnp.concatenate([peer_own, kv_own], axis=0)
    block_count = tokens // Q_BLOCK
    block_numbers = jnp.arange(block_count, dtype=jnp.int32)
    high = (row_offset + (block_numbers + 1) * Q_BLOCK) // K_BLOCK
    prefix_end = jnp.minimum((prefix + K_BLOCK - 1) // K_BLOCK, high)
    low = jnp.maximum(starts[::Q_BLOCK] // K_BLOCK, prefix_end)
    blocks = jnp.stack([prefix_end, low, high])
    info = jnp.stack([row_offset, prefix, (1 - tp) * tokens])

    page_count = group_len // PAGE
    lane_count = -(-page_count // req_count)
    page_numbers = jnp.arange(page_count, dtype=jnp.int32)
    live_pages = segment_ids[::PAGE] != REQS + 1
    half_pages = page_count // 2
    swap = lambda x: jnp.where(tp == 0, jnp.roll(x, half_pages), x)
    local_numbers, local_owner, local_live = swap(page_numbers), swap(page_owner), swap(live_pages)
    page_data = (
        cached.reshape(page_count, PAGE, 2, local_kv, HEAD)
        .transpose(0, 3, 2, 1, 4)
        .reshape(page_count, local_kv * 2 * PAGE * HEAD)
    )
    same_owner = (
        (local_owner[:, None] == local_owner[None, :])
        & local_live[None, :]
        & (local_numbers[None, :] < local_numbers[:, None])
    )
    page_rank = jnp.sum(same_owner.astype(jnp.int32), axis=1)
    owner_ids = jnp.arange(req_count, dtype=jnp.int32)
    lane_ids = jnp.arange(lane_count, dtype=jnp.int32)
    selection = (
        (local_owner[None, None, :] == owner_ids[:, None, None])
        & (page_rank[None, None, :] == lane_ids[None, :, None])
        & local_live[None, None, :]
    )
    send_pages = jnp.einsum(
        "olp,pc->olc", selection.astype(jnp.bfloat16), page_data, preferred_element_type=jnp.float32
    ).astype(jnp.bfloat16)
    send_ids = jnp.sum(jnp.where(selection, local_numbers[None, None, :] + 1, 0), axis=2) - 1
    received_ids = lax.all_to_all(send_ids, "req", split_axis=0, concat_axis=0, tiled=True)
    received = lax.all_to_all(send_pages, "req", split_axis=0, concat_axis=0, tiled=True)
    hidden_out = attention(info, blocks, queries, keys_values, starts[:, None], w_out, wo_other, hidden_in)
    placing = (
        received_ids.reshape(req_count * lane_count)[None, :] == page_numbers[:, None]
    ).astype(jnp.bfloat16)
    cache_rows = jnp.dot(
        placing,
        received.reshape(req_count * lane_count, local_kv * 2 * PAGE * HEAD),
        preferred_element_type=jnp.float32,
    ).astype(jnp.bfloat16)
    return (hidden_out, cache_rows.reshape(page_count, local_kv, 2, PAGE * HEAD))


def solution(mesh):
    placed = (P(("req", "tp"), None), P("req"), P("req"), P(), P(None, "tp"), P("tp", None))
    return jax.shard_map(
        shards,
        mesh=mesh,
        in_specs=placed,
        out_specs=(P(("req", "tp"), None), P("req", "tp", None, None)),
        check_vma=False,
    )
```

```python
import jax
import jax.numpy as jnp
from jax import lax
from jax.experimental import pallas as pl
from jax.experimental.pallas import tpu as pltpu
from jax.sharding import PartitionSpec as P

HEAD = 96
HEADS_Q = 8
HEADS_KV = 4
PAGE = 64
REQS = 8


rotary_base = 100000.0
norm_eps = 1e-05
masked_score = -1e30


def rotary_tables(positions, width):
    half_width = width // 2
    exponent = jnp.arange(half_width, dtype=jnp.float32) * (2.0 / width)
    inverse = jnp.power(jnp.float32(rotary_base), -exponent)
    angles = positions.astype(jnp.float32)[:, None] * inverse[None, :]
    return (jnp.cos(angles), jnp.sin(angles))


def normalize(token_rows, gain_vector):
    values = token_rows.astype(jnp.float32)
    inverse_root = lax.rsqrt(jnp.mean(values * values, axis=-1, keepdims=True) + norm_eps)
    return (values * inverse_root * gain_vector.astype(jnp.float32)).astype(jnp.bfloat16)


Q_BLOCK = 256
K_BLOCK = 256
PIECES = 3
LANES = 128


def project_kernel(
    hidden_ref, gain_ref, cosine_ref, sine_ref, wq_ref, wo_ref,
    q_own_ref, kv_own_ref, q_other_ref, kv_other_ref, wo_other_ref, peer_own_ref,
    wq_other_ref, normed_ref, cos_ref, left_ref, right_ref, send_sem, recv_sem, kv_send, kv_recv,
):
    req = lax.axis_index("req")
    tp = lax.axis_index("tp")
    member = lax.rem(req, 4)
    base = req - member
    core_member = member + 1 - 2 * lax.rem(member, 2)
    row_member = member + 2 - 4 * (member // 2)
    across = {"tp": 1 - tp}
    core_peer = {"req": base + core_member}
    row_peer = {"req": base + row_member}
    barrier = pltpu.get_barrier_semaphore()
    for peer in (across, core_peer, row_peer):
        pl.semaphore_signal(barrier, inc=1, device_id=peer, device_id_type=pl.DeviceIdType.MESH)
    pl.semaphore_wait(barrier, 3)

    q_rows = wq_ref.shape[0] // 4 // PIECES
    o_rows = wo_ref.shape[0] // 4

    def remote(src, dst, sends, receives, peer):
        return pltpu.make_async_remote_copy(
            src_ref=src, dst_ref=dst, send_sem=sends, recv_sem=receives,
            device_id=peer, device_id_type=pl.DeviceIdType.MESH,
        )

    def views(ref_q, ref_o, owner, piece):
        if piece < PIECES:
            return ref_q.at[pl.ds((owner * PIECES + piece) * q_rows, q_rows)]
        return ref_o.at[pl.ds(owner * o_rows, o_rows)]

    def copy(source, owner, piece, channel, peer):
        return remote(
            views(*source, owner, piece), views(wq_other_ref, wo_other_ref, owner, piece),
            send_sem.at[piece, channel], recv_sem.at[piece, channel], peer,
        )

    here = (wq_other_ref, wo_other_ref)
    pieces = range(PIECES + 1)
    first = [copy((wq_ref, wo_ref), member, p, 0, across) for p in pieces]
    core_first = [copy(here, member, p, 1, core_peer) for p in pieces]
    row_first = [copy(here, member, p, 2, row_peer) for p in pieces]
    core_second = [copy(here, row_member, p, 3, core_peer) for p in pieces]
    tokens = hidden_ref.shape[0]
    blocks = tokens // Q_BLOCK
    width = cos_ref.shape[1]
    half = HEAD // 2

    def kv_copy(source, target, which, block):
        rows = pl.ds(block * Q_BLOCK, Q_BLOCK)
        return remote(
            source.at[rows], target.at[rows], kv_send.at[which, block], kv_recv.at[which, block], across
        )

    other_copies = [kv_copy(kv_other_ref, peer_own_ref, 0, b) for b in range(blocks)]

    for p in range(PIECES):
        first[p].start()

    def project(rows, weight_ref, q_ref, kv_ref):
        normed = normed_ref[rows, :]
        cosine, left, right = cos_ref[rows, :], left_ref[rows, :], right_ref[rows, :]

        def turn(x):
            return (
                x * cosine
                + pltpu.roll(x, width - half, 1) * left
                + pltpu.roll(x, half, 1) * right
            )

        q = jnp.dot(normed, weight_ref[:, :width], preferred_element_type=jnp.float32)
        q_ref[rows, :] = turn(q).astype(jnp.bfloat16)
        kv = jnp.dot(normed, weight_ref[:, width:], preferred_element_type=jnp.float32)
        lanes = lax.broadcasted_iota(jnp.int32, kv.shape, 1)
        kv_ref[rows, :] = jnp.where(lanes < width // 2, turn(kv), kv).astype(jnp.bfloat16)

    def own(block):
        rows = pl.ds(block * Q_BLOCK, Q_BLOCK)
        normed_ref[rows, :] = normalize(hidden_ref[rows, :], gain_ref[...])
        cosine, sine = cosine_ref[rows, :], sine_ref[rows, :]
        nothing = jnp.zeros_like(sine)
        for piece in range(width // half):
            lanes = slice(piece * half, (piece + 1) * half)
            cos_ref[rows, lanes] = cosine
            left_ref[rows, lanes] = nothing if piece % 2 else -sine
            right_ref[rows, lanes] = sine if piece % 2 else nothing
        project(rows, wq_ref, q_own_ref, kv_own_ref)

    def forward(p):
        first[p].wait_recv()
        row_first[p].start()
        core_first[p].start()

    for block in range(blocks):
        own(block)
        if block >= 1:
            forward(block - 1)
    first[PIECES].start()
    for p in range(PIECES):
        row_first[p].wait_recv()
        core_second[p].start()
    for p in range(PIECES):
        core_first[p].wait_recv()
        core_second[p].wait_recv()
    for block in range(blocks):
        project(pl.ds(block * Q_BLOCK, Q_BLOCK), wq_other_ref, q_other_ref, kv_other_ref)
        other_copies[block].start()
        if block == 1:
            forward(PIECES)
    row_first[PIECES].wait_recv()
    core_second[PIECES].start()
    core_first[PIECES].wait_recv()
    core_second[PIECES].wait_recv()
    for p in pieces:
        for c in (first[p], row_first[p], core_first[p], core_second[p]):
            c.wait_send()
    for c in other_copies:
        c.wait()


def project(hidden, gain, cosine, sine, w_qkv, w_out):
    tokens, width = hidden.shape
    part = w_qkv.shape[1] // 2
    blocks = tokens // Q_BLOCK
    vmem = pl.BlockSpec(memory_space=pltpu.VMEM)
    anywhere = pl.BlockSpec(memory_space=pl.ANY)
    share = jax.ShapeDtypeStruct((tokens, part), jnp.bfloat16)
    return pl.pallas_call(
        project_kernel,
        out_shape=(share,) * 4 + (jax.ShapeDtypeStruct(w_out.shape, w_out.dtype), share),
        in_specs=[vmem] * 5 + [anywhere],
        out_specs=[vmem] * 4 + [anywhere] * 2,
        scratch_shapes=[
            pltpu.VMEM(w_qkv.shape, w_qkv.dtype),
            pltpu.VMEM((tokens, width), jnp.bfloat16),
            pltpu.VMEM((tokens, part), jnp.float32),
            pltpu.VMEM((tokens, part), jnp.float32),
            pltpu.VMEM((tokens, part), jnp.float32),
            pltpu.SemaphoreType.DMA((PIECES + 1, 4)),
            pltpu.SemaphoreType.DMA((PIECES + 1, 4)),
            pltpu.SemaphoreType.DMA((1, blocks)),
            pltpu.SemaphoreType.DMA((1, blocks)),
        ],
        compiler_params=pltpu.CompilerParams(
            collective_id=0, has_side_effects=True, vmem_limit_bytes=48 * 1024 * 1024
        ),
        cost_estimate=pl.CostEstimate(
            flops=5_000_000_000, bytes_accessed=16_000_000, transcendentals=1024
        ),
        name="project",
    )(hidden, gain, cosine, sine, w_qkv, w_out)


def attention_kernel(
    info_ref, blocks_ref, q_own_ref, q_other_ref, peer_own_ref, kv_own_ref, peer_other_ref, kv_other_ref,
    starts_ref, wo_own_ref, wo_other_ref, hidden_ref, out_ref, mixed_ref, kv_ref
):
    block = pl.program_id(0)

    @pl.when(block == 0)
    def _():
        tokens = kv_own_ref.shape[0]
        extra = lax.broadcasted_iota(jnp.int32, (2 * tokens, LANES - HEAD), 1)
        extra = jnp.where(extra == 0, 1.0, 0.0).astype(jnp.bfloat16)
        for row in (2, 3, 6, 7):
            kv_ref[row, :, HEAD:] = extra
        sources = ((peer_own_ref, kv_own_ref), (peer_other_ref, kv_other_ref))
        for group in range(2):
            for part in range(2):
                for head in range(4):
                    kv_ref[group * 4 + head, part * tokens : (part + 1) * tokens, :HEAD] = sources[group][
                        part
                    ][:, head * HEAD : (head + 1) * HEAD]

    row_offset = info_ref[0]
    prefix = info_ref[1]
    key_offset = info_ref[2]
    prefix_end = blocks_ref[0, block]
    low = blocks_ref[1, block]
    high = blocks_ref[2, block]
    factor = HEAD ** (-0.5) * 1.4426950408889634
    local = lax.broadcasted_iota(jnp.int32, (Q_BLOCK, 1), 0) + row_offset + block * Q_BLOCK
    places = jnp.concatenate([local, local], axis=0)
    starts = starts_ref[...]
    starts = jnp.concatenate([starts, starts], axis=0)
    queries = []
    for head in range(HEADS_KV):
        q_ref = q_own_ref if head < 2 else q_other_ref
        lane = (head % 2) * 2 * HEAD
        queries.append(
            jnp.concatenate(
                [q_ref[:, lane : lane + HEAD], q_ref[:, lane + HEAD : lane + 2 * HEAD]], axis=0
            )
        )

    def step(number, carry):
        begin = pl.multiple_of(number * K_BLOCK + key_offset, K_BLOCK)
        key_places = lax.broadcasted_iota(jnp.int32, (1, K_BLOCK), 1) + number * K_BLOCK
        allowed = (key_places <= places) & ((key_places >= starts) | (key_places < prefix))
        after = []
        for head in range(HEADS_KV):
            key_row = (head // 2) * 4 + head % 2
            row_max, mixed = carry[head]
            keys = kv_ref[key_row, pl.ds(begin, K_BLOCK), :HEAD]
            values = kv_ref[key_row + 2, pl.ds(begin, K_BLOCK), :]
            scores = lax.dot_general(
                queries[head], keys, (((1,), (1,)), ((), ())), preferred_element_type=jnp.float32
            ) * factor
            scores = jnp.where(allowed, scores, masked_score)
            new_max = jnp.maximum(row_max, jnp.max(scores, axis=1, keepdims=True))
            weights = jnp.exp2(scores - new_max).astype(jnp.bfloat16)
            scale = jnp.exp2(row_max - new_max)
            mixed = mixed * scale + jnp.dot(weights, values, preferred_element_type=jnp.float32)
            after.append((new_max, mixed))
        return tuple(after)

    carry = tuple(
        (
            jnp.full((2 * Q_BLOCK, 1), -1e20, jnp.float32),
            jnp.zeros((2 * Q_BLOCK, LANES), jnp.float32),
        )
        for _ in range(HEADS_KV)
    )
    carry = lax.fori_loop(0, prefix_end, step, carry)
    carry = lax.fori_loop(low, high, step, carry)
    for head in range(HEADS_KV):
        mixed = carry[head][1]
        result = (mixed[:, :HEAD] / mixed[:, HEAD : HEAD + 1]).astype(jnp.bfloat16)
        mixed_ref[:, 2 * head * HEAD : (2 * head + 1) * HEAD] = result[:Q_BLOCK]
        mixed_ref[:, (2 * head + 1) * HEAD : (2 * head + 2) * HEAD] = result[Q_BLOCK:]
    half = HEADS_Q * HEAD // 2
    product = jnp.dot(mixed_ref[:, :half], wo_own_ref[...], preferred_element_type=jnp.float32)
    product += jnp.dot(mixed_ref[:, half:], wo_other_ref[...], preferred_element_type=jnp.float32)
    out_ref[...] = (hidden_ref[...].astype(jnp.float32) + product).astype(jnp.bfloat16)


def attention(info, blocks, queries, keys_values, starts, wo_own, wo_other, hidden):
    tokens, width = hidden.shape
    half = queries[0].shape[1]
    whole = lambda shape: pl.BlockSpec(shape, lambda i, *_: (0,) * len(shape))
    return pl.pallas_call(
        attention_kernel,
        grid_spec=pltpu.PrefetchScalarGridSpec(
            num_scalar_prefetch=2,
            grid=(tokens // Q_BLOCK,),
            in_specs=[
                pl.BlockSpec((Q_BLOCK, half), lambda i, *_: (i, 0)),
                pl.BlockSpec((Q_BLOCK, half), lambda i, *_: (i, 0)),
                whole((tokens, half)),
                whole((tokens, half)),
                whole((tokens, half)),
                whole((tokens, half)),
                pl.BlockSpec((Q_BLOCK, 1), lambda i, *_: (i, 0)),
                whole(wo_own.shape),
                whole(wo_other.shape),
                pl.BlockSpec((Q_BLOCK, width), lambda i, *_: (i, 0)),
            ],
            out_specs=pl.BlockSpec((Q_BLOCK, width), lambda i, *_: (i, 0)),
            scratch_shapes=[
                pltpu.VMEM((Q_BLOCK, HEADS_Q * HEAD), jnp.bfloat16),
                pltpu.VMEM((2 * HEADS_KV, 2 * tokens, LANES), jnp.bfloat16),
            ],
        ),
        out_shape=jax.ShapeDtypeStruct(hidden.shape, hidden.dtype),
        compiler_params=pltpu.CompilerParams(vmem_limit_bytes=48 * 1024 * 1024),
        cost_estimate=pl.CostEstimate(
            flops=20_000_000_000, bytes_accessed=16_000_000, transcendentals=8_000_000
        ),
        name="attention",
    )(info, blocks, *queries, *keys_values, starts, wo_own, wo_other, hidden)


def shards(hidden_in, segment_ids, page_owner, norm_gain, w_qkv, w_out):
    req_count = lax.axis_size("req")
    tp = lax.axis_index("tp")
    group_len = segment_ids.shape[0]
    tokens = hidden_in.shape[0]
    local_kv = HEADS_KV // 2
    row_offset = tp * tokens
    numbers = jnp.arange(REQS + 2, dtype=jnp.int32)
    firsts = jnp.sum((segment_ids[None, :] < numbers[:, None]).astype(jnp.int32), axis=1)
    prefix = firsts[1]
    own_segments = lax.dynamic_slice(segment_ids, (row_offset,), (tokens,))
    starts = jnp.sum(
        jnp.where(own_segments[:, None] == numbers[None, :], firsts[None, :], 0), axis=1
    )
    places = row_offset + jnp.arange(tokens, dtype=jnp.int32)
    positions = places - starts + jnp.where(own_segments > 0, prefix, 0)
    cosine, sine_table = rotary_tables(positions, HEAD)
    q_own, kv_own, q_other, kv_other, wo_other, peer_own = project(
        hidden_in, norm_gain[None, :], cosine, sine_table, w_qkv, w_out
    )
    peer_other = lax.ppermute(kv_own, "tp", [(0, 1)])
    queries = (q_own, q_other)
    cached = jnp.concatenate([peer_own, kv_own], axis=0)
    block_count = tokens // Q_BLOCK
    block_numbers = jnp.arange(block_count, dtype=jnp.int32)
    high = (row_offset + (block_numbers + 1) * Q_BLOCK) // K_BLOCK
    prefix_end = jnp.minimum((prefix + K_BLOCK - 1) // K_BLOCK, high)
    low = jnp.maximum(starts[::Q_BLOCK] // K_BLOCK, prefix_end)
    blocks = jnp.stack([prefix_end, low, high])
    info = jnp.stack([row_offset, prefix, (1 - tp) * tokens])

    page_count = group_len // PAGE
    lane_count = -(-page_count // req_count)
    page_numbers = jnp.arange(page_count, dtype=jnp.int32)
    live_pages = segment_ids[::PAGE] != REQS + 1
    half_pages = page_count // 2
    swap = lambda x: jnp.where(tp == 0, jnp.roll(x, half_pages), x)
    local_numbers, local_owner, local_live = swap(page_numbers), swap(page_owner), swap(live_pages)
    page_data = (
        cached.reshape(page_count, PAGE, 2, local_kv, HEAD)
        .transpose(0, 3, 2, 1, 4)
        .reshape(page_count, local_kv * 2 * PAGE * HEAD)
    )
    same_owner = (
        (local_owner[:, None] == local_owner[None, :])
        & local_live[None, :]
        & (local_numbers[None, :] < local_numbers[:, None])
    )
    page_rank = jnp.sum(same_owner.astype(jnp.int32), axis=1)
    owner_ids = jnp.arange(req_count, dtype=jnp.int32)
    lane_ids = jnp.arange(lane_count, dtype=jnp.int32)
    selection = (
        (local_owner[None, None, :] == owner_ids[:, None, None])
        & (page_rank[None, None, :] == lane_ids[None, :, None])
        & local_live[None, None, :]
    )
    send_pages = jnp.einsum(
        "olp,pc->olc", selection.astype(jnp.bfloat16), page_data, preferred_element_type=jnp.float32
    ).astype(jnp.bfloat16)
    send_pages, peer_other = lax.optimization_barrier((send_pages, peer_other))
    keys_values = (peer_own, kv_own, peer_other, kv_other)
    send_ids = jnp.sum(jnp.where(selection, local_numbers[None, None, :] + 1, 0), axis=2) - 1
    received_ids = lax.all_to_all(send_ids, "req", split_axis=0, concat_axis=0, tiled=True)
    received = lax.all_to_all(send_pages, "req", split_axis=0, concat_axis=0, tiled=True)
    hidden_out = attention(info, blocks, queries, keys_values, starts[:, None], w_out, wo_other, hidden_in)
    placing = (
        received_ids.reshape(req_count * lane_count)[None, :] == page_numbers[:, None]
    ).astype(jnp.bfloat16)
    cache_rows = jnp.dot(
        placing,
        received.reshape(req_count * lane_count, local_kv * 2 * PAGE * HEAD),
        preferred_element_type=jnp.float32,
    ).astype(jnp.bfloat16)
    return (hidden_out, cache_rows.reshape(page_count, local_kv, 2, PAGE * HEAD))


def solution(mesh):
    placed = (P(("req", "tp"), None), P("req"), P("req"), P(), P(None, "tp"), P("tp", None))
    return jax.shard_map(
        shards,
        mesh=mesh,
        in_specs=placed,
        out_specs=(P(("req", "tp"), None), P("req", "tp", None, None)),
        check_vma=False,
    )
```
